32 devices in a mesh: groups: 2 (over y), loop: 4 (over z), dp: 2 (over x), fsdp: 2 (over core).
Axes of the slice: x: 2, y: 2, z: 4, core: 2. Of those that a mesh axis runs over, the one named last changes fastest.
Arguments:
- activations: bfloat16 [768, 5120], P(('groups', 'dp')), parts along dimension 0, may hold values from -6 to 6
- cotangent: bfloat16 [768, 5120], P(('groups', 'dp')), parts along dimension 0, may hold values from -6 to 6
- weights_in: bfloat16 [864, 2, 5120], P(('loop', 'fsdp'), None, 'dp'), may hold values from -0.078125 to 0.078125
- weights_down: bfloat16 [864, 5120], P(('loop', 'fsdp'), 'dp'), may hold values from -0.21875 to 0.21875
- norm_gains: float32 [5120], replicated, may hold values from 0.1 to 1.9
Outputs:
- grad_in: float32 [1728, 2, 5120], P(('groups', 'loop', 'fsdp'), None, 'dp'), parts along dimension 0
- grad_down: float32 [1728, 5120], P(('groups', 'loop', 'fsdp'), 'dp'), parts along dimension 0
- grad_gains: float32 [10240], P('groups'), parts along dimension 0
- grad_act: bfloat16 [768, 5120], P(('groups', 'dp')), parts along dimension 0
The draws below stay inside these ranges and needn't reach their ends.
There are 2 independent parts, one for each index of `groups`. The reference program is written for one: setup_inputs(seed, part) draws one part's arguments, and reference() takes and returns one part's arrays. A program takes and returns all parts, laid end to end along the dimension named above; an argument that names none is the same for every part. Nothing has to cross between parts.
All inputs are finite; a program needn't handle non-finite values.
Results may differ from the reference program's by a relative error of at most 0.0065.
Values may be sent and summed in bfloat16 or wider, within the bound.
A program may use at most 64 MiB of HBM per device.

```python
import jax
import jax.numpy as jnp
from jax import lax

D = 5120
TOK = 192
FW = 864
TOKENS = 384


def steps_of(stream_key, dims, split, least, high):
    gain = 1.0
    for position, shards_of in split:
        heights = jax.random.uniform(jax.random.fold_in(jax.random.fold_in(stream_key, 6), position), (shards_of,), jnp.float32, least / len(split), high / len(split))
        gain = gain * jnp.repeat(jnp.exp(heights), dims[position] // shards_of).reshape((-1,) + (1,) * (len(dims) - 1 - position))
    return gain


def bell_draw(own_key, shape, spread, bound, pieces=(), held_as=jnp.bfloat16):
    result = spread * jax.random.normal(own_key, shape, jnp.float32)
    if pieces:
        result = result * steps_of(own_key, shape, pieces, -0.22, 0.18)
    return jnp.clip(result, -bound, bound).astype(held_as)


def setup_inputs(seed: int = 0, part: int = 0) -> dict:
    keys = jax.random.split(jax.random.key(seed), 6)
    own_keys = jax.random.split(jax.random.fold_in(keys[5], part), 6)
    activations = bell_draw(own_keys[0], (TOKENS, D), 1.0, 6.0, ((0, 2),))
    cotangent = bell_draw(own_keys[1], (TOKENS, D), 1.0, 6.0, ((0, 2),))
    weights_in = bell_draw(keys[2], (FW, 2, D), D ** -0.5, 0.078125, ((0, 8), (2, 2)))
    weights_down = bell_draw(keys[3], (FW, D), FW ** -0.5, 0.21875, ((0, 8), (1, 2)))
    norm_gains = jnp.clip(1.0 + 0.18 * jax.random.normal(keys[4], (D,), jnp.float32), 0.1, 1.9)
    return dict(activations=activations, cotangent=cotangent, weights_in=weights_in, weights_down=weights_down, norm_gains=norm_gains)


EPSILON = 1e-05

def contract_rows(left, right):
    return lax.dot_general(left, right, (((0,), (0,)), ((), ())), preferred_element_type=jnp.float32)

def reference(activations, cotangent, weights_in, weights_down, norm_gains):
    x_float = activations.astype(jnp.float32)
    inv_rms = lax.rsqrt(lax.optimization_barrier(jnp.mean(x_float * x_float, axis=-1, keepdims=True)) + EPSILON)
    x_hat = x_float * inv_rms
    normed = (x_hat * norm_gains).astype(jnp.bfloat16)
    gate_val = jnp.dot(normed, weights_in[:, 0, :].T, preferred_element_type=jnp.float32)
    up_val = jnp.dot(normed, weights_in[:, 1, :].T, preferred_element_type=jnp.float32)
    sigma = jax.nn.sigmoid(gate_val)
    silu_val = gate_val * sigma
    hidden = (silu_val * up_val).astype(jnp.bfloat16)
    grad_b = cotangent
    d_hidden = jnp.dot(grad_b, weights_down.T, preferred_element_type=jnp.float32)
    d_gate = (d_hidden * up_val * sigma * (1.0 + gate_val * (1.0 - sigma))).astype(jnp.bfloat16)
    d_up = (d_hidden * silu_val).astype(jnp.bfloat16)
    d_normed = jnp.dot(d_gate, weights_in[:, 0, :], preferred_element_type=jnp.float32) + jnp.dot(d_up, weights_in[:, 1, :], preferred_element_type=jnp.float32)
    grad_gains = lax.optimization_barrier(jnp.sum(d_normed * x_hat, axis=0))
    scaled = d_normed * norm_gains
    grad_act = (cotangent.astype(jnp.float32) + inv_rms * (scaled - x_hat * lax.optimization_barrier(jnp.mean(scaled * x_hat, axis=-1, keepdims=True)))).astype(jnp.bfloat16)
    totals = jnp.zeros((FW, 3, D), jnp.float32)
    for block in range(TOKENS // TOK):
        lo = block * TOK
        term = jnp.stack([contract_rows(d_gate[lo:lo + TOK], normed[lo:lo + TOK]), contract_rows(d_up[lo:lo + TOK], normed[lo:lo + TOK]), contract_rows(hidden[lo:lo + TOK], grad_b[lo:lo + TOK])], axis=1)
        totals = totals + lax.optimization_barrier(term.astype(jnp.bfloat16)).astype(jnp.float32)
    return (totals[:, 0:2, :], totals[:, 2, :], grad_gains, grad_act)
```

```python
import functools

import jax
import jax.numpy as jnp
from jax import lax
from jax.experimental import pallas as pl
from jax.experimental.pallas import tpu as pltpu
from jax.sharding import PartitionSpec as P

EPSILON = 1e-05


def contract_rows(left, right):
    return lax.dot_general(
        left, right, (((0,), (0,)), ((), ())), preferred_element_type=jnp.float32
    )


def input_grad(d_normed, x_hat, inv_rms, cotangent, norm_gains):
    scaled = d_normed * norm_gains
    return (
        cotangent.astype(jnp.float32)
        + inv_rms * (scaled - x_hat * jnp.mean(scaled * x_hat, axis=-1, keepdims=True))
    ).astype(jnp.bfloat16)


def on_device(activations, cotangent, weights_in, weights_down, norm_gains):
    x_float = activations.astype(jnp.float32)
    inv_rms = lax.rsqrt(jnp.mean(x_float * x_float, axis=-1, keepdims=True) + EPSILON)
    x_hat = x_float * inv_rms
    normed = (x_hat * norm_gains).astype(jnp.bfloat16)
    full_in, full_down = (
        lax.all_gather(weights_in, "dp", axis=2, tiled=True),
        lax.all_gather(weights_down, "dp", axis=1, tiled=True),
    )
    gate_val = jnp.dot(normed, full_in[:, 0, :].T, preferred_element_type=jnp.float32)
    up_val = jnp.dot(normed, full_in[:, 1, :].T, preferred_element_type=jnp.float32)
    d_hidden = jnp.dot(cotangent, full_down.T, preferred_element_type=jnp.float32)
    sigma = jax.nn.sigmoid(gate_val)
    silu_val = gate_val * sigma
    hidden = (silu_val * up_val).astype(jnp.bfloat16)
    d_gate = (d_hidden * up_val * sigma * (1.0 + gate_val * (1.0 - sigma))).astype(jnp.bfloat16)
    d_up = (d_hidden * silu_val).astype(jnp.bfloat16)
    partial_normed = jnp.dot(
        d_gate, full_in[:, 0, :], preferred_element_type=jnp.float32
    ) + jnp.dot(d_up, full_in[:, 1, :], preferred_element_type=jnp.float32)
    d_normed = lax.psum(partial_normed, ("loop", "fsdp"))
    grad_gains = lax.psum(jnp.sum(d_normed * x_hat, axis=0), "dp")
    grad_act = input_grad(d_normed, x_hat, inv_rms, cotangent, norm_gains)
    term = jnp.stack(
        [
            contract_rows(d_gate, normed),
            contract_rows(d_up, normed),
            contract_rows(hidden, cotangent),
        ],
        axis=1,
    )
    term = lax.optimization_barrier(term.astype(jnp.bfloat16)).astype(jnp.float32)
    summed = lax.psum_scatter(
        term.astype(jnp.bfloat16), "dp", scatter_dimension=2, tiled=True
    ).astype(jnp.float32)
    return (summed[:, 0:2, :], summed[:, 2, :], grad_gains, grad_act)


HP = 128


def dot_t(left, right):
    return lax.dot_general(
        left, right, (((1,), (1,)), ((), ())), preferred_element_type=jnp.float32
    )


def fused_kernel(
    L, act, cot, wgu, wd, gains,
    g_gate, g_up, g_down, g_gains, out,
    normed, xhat, inv_s, cotf, tok_x, part, part_x, dgu, hid,
    dn, p_buf, r_buf, qf, q_buf, rz, t_buf, t_x, fin, gsum, gx, gc, gz,
    s_x, r_x, s_c, r_c, s_p, r_p, s_d, r_d, s_z, r_z, s_t, r_t,
    s_ag, r_ag, s_fw, r_fw, s_g, r_g, s_gz, r_gz,
):
    tok, width = act.shape
    half = width // 2
    hb = tok // 2
    ch = tok // (2 * L)
    l, d, f = lax.axis_index("loop"), lax.axis_index("dp"), lax.axis_index("fsdp")
    mine = pl.ds(pl.multiple_of(d * half, 128), half)
    theirs = pl.ds(pl.multiple_of((1 - d) * half, 128), half)
    x_dev, c_dev = {"dp": 1 - d}, {"fsdp": 1 - f}
    to = [lax.rem(l + k, L) for k in range(L)]
    frm = [lax.rem(l - k + L, L) for k in range(L)]

    def rc(src, dst, ss, rs, dev):
        return pltpu.make_async_remote_copy(
            src_ref=src, dst_ref=dst, send_sem=ss, recv_sem=rs,
            device_id=dev, device_id_type=pl.DeviceIdType.MESH,
        )

    barrier = pltpu.get_barrier_semaphore()
    for dev in [x_dev, c_dev] + [{"loop": to[k]} for k in range(1, L)]:
        pl.semaphore_signal(barrier, inc=1, device_id=dev, device_id_type=pl.DeviceIdType.MESH)
    pl.semaphore_wait(barrier, L + 1)

    my_rows = pl.ds(pl.multiple_of(f * hb, 16), hb)
    x_cot = rc(cot.at[my_rows, theirs], tok_x.at[1, my_rows], s_x.at[1], r_x.at[1], x_dev)
    x_cot.start()

    def norm_rows(start):
        def body(i, carry):
            rows = pl.ds(pl.multiple_of(start + i * 16, 16), 16)
            x = act[rows, :].astype(jnp.float32)
            inv = lax.rsqrt(jnp.mean(x * x, axis=-1, keepdims=True) + EPSILON)
            xh = x * inv
            xhat[rows, :] = xh
            inv_s[rows, :] = jnp.broadcast_to(inv, (16, 128))
            normed[rows, :] = (xh * gains[...]).astype(jnp.bfloat16)
            return carry

        lax.fori_loop(0, hb // 16, body, 0)

    norm_rows(f * hb)
    x_nrm = rc(normed.at[my_rows, theirs], tok_x.at[0, my_rows], s_x.at[0], r_x.at[0], x_dev)
    x_nrm.start()
    norm_rows((1 - f) * hb)

    part[0, 2] = dot_t(cot[:, mine], wd[...])
    gu = dot_t(normed[:, mine], wgu[...])
    part[0, 0] = gu[:, :HP]
    part[0, 1] = gu[:, HP:]
    part_x[0] = part[0].astype(jnp.bfloat16)
    p_own = rc(part_x.at[0], part_x.at[3], s_p.at[0], r_p.at[0], x_dev)
    p_own.start()

    def cot_body(i, carry):
        rows = pl.ds(pl.multiple_of(i * 16, 16), 16)
        cotf[rows, :] = cot[rows, :].astype(jnp.float32)
        return carry

    lax.fori_loop(0, tok // 16, cot_body, 0)

    x_cot.wait()
    c_cot = rc(tok_x.at[1, my_rows], tok_x.at[1, my_rows], s_c.at[1], r_c.at[1], c_dev)
    c_cot.start()
    x_nrm.wait()
    c_nrm = rc(tok_x.at[0, my_rows], tok_x.at[0, my_rows], s_c.at[0], r_c.at[0], c_dev)
    c_nrm.start()
    c_cot.wait()
    part[1, 2] = dot_t(tok_x[1], wd[...])
    c_nrm.wait()
    gu = dot_t(tok_x[0], wgu[...])
    part[1, 0] = gu[:, :HP]
    part[1, 1] = gu[:, HP:]
    part_x[1] = part[1].astype(jnp.bfloat16)
    p_oth = rc(part_x.at[1], part_x.at[2], s_p.at[1], r_p.at[1], x_dev)
    p_oth.start()

    def hidden_grads(t):
        gate = part[t, 0] + part_x[2 + t, 0].astype(jnp.float32)
        up = part[t, 1] + part_x[2 + t, 1].astype(jnp.float32)
        dh = part[t, 2] + part_x[2 + t, 2].astype(jnp.float32)
        sig = jax.nn.sigmoid(gate)
        silu = gate * sig
        hid[t] = (silu * up).astype(jnp.bfloat16)
        dgu[t, :, :HP] = (dh * up * sig * (1.0 + gate * (1.0 - sig))).astype(jnp.bfloat16)
        dgu[t, :, HP:] = (dh * silu).astype(jnp.bfloat16)

        def body(i, carry):
            cols = pl.ds(pl.multiple_of(i * 512, 128), 512)
            dn[t, :, cols] = jnp.dot(
                dgu[t], wgu[:, cols], preferred_element_type=jnp.float32
            )
            return carry

        lax.fori_loop(0, half // 512, body, 0)
        for j in range(L):
            rows = pl.ds(pl.multiple_of((2 * j + 1 - f) * ch, 8), ch)
            p_buf[t, j] = dn[t, rows, :].astype(jnp.bfloat16)
        copy = rc(p_buf.at[t], r_buf.at[t], s_d.at[t], r_d.at[t], c_dev)
        copy.start()
        return copy

    p_own.wait()
    d1 = hidden_grads(1)
    p_oth.wait()
    d0 = hidden_grads(0)

    zc = {}
    for t, dd in ((1, d1), (0, d0)):
        dd.wait()
        for k in (L // 2, *[k for k in range(1, L) if k != L // 2], 0):
            rows = pl.ds(pl.multiple_of((2 * to[k] + f) * ch, 8), ch)
            val = dn[t, rows, :] + r_buf[t, to[k]].astype(jnp.float32)
            if k == 0:
                qf[t] = val
            else:
                q_buf[k, t] = val.astype(jnp.bfloat16)
                zc[k, t] = rc(q_buf.at[k, t], rz.at[k, t], s_z.at[k, t], r_z.at[k, t], {"loop": to[k]})
                zc[k, t].start()

    def wg_body(i, carry):
        cols = pl.ds(pl.multiple_of(i * 256, 128), 256)
        own = pl.ds(pl.multiple_of(d * half + i * 256, 128), 256)
        gu = contract_rows(dgu[0], normed[:, own]) + contract_rows(dgu[1], tok_x[0, :, cols])
        rows = g_gate.shape[0]
        g_gate[:, cols] = gu[:rows]
        g_up[:, cols] = gu[HP : HP + rows]
        down = contract_rows(hid[0], cot[:, own]) + contract_rows(hid[1], tok_x[1, :, cols])
        g_down[:, cols] = down[:rows]
        return carry

    lax.fori_loop(0, half // 256, wg_body, 0)

    def total(t):
        for k in range(1, L):
            zc[k, t].wait()
        val = qf[t]
        for k in range(1, L):
            val = val + rz[k, t].astype(jnp.float32)
        return val

    t_buf[...] = total(1).astype(jnp.bfloat16)
    tc = rc(t_buf, t_x, s_t.at[0], r_t.at[0], x_dev)
    tc.start()
    fin[:, mine] = total(0)
    tc.wait()
    fin[:, theirs] = t_x[...].astype(jnp.float32)

    rows = pl.ds(pl.multiple_of((2 * l + f) * ch, 8), ch)
    dnf = fin[...]
    xh = xhat[rows, :]
    scaled = dnf * gains[...]
    mean = jnp.mean(scaled * xh, axis=-1, keepdims=True)
    res = cotf[rows, :] + inv_s[rows, :1] * (scaled - xh * mean)
    slot = 2 * l + f
    out[slot] = res.astype(jnp.bfloat16)
    ag = {}
    for k in (L // 2, *[k for k in range(1, L) if k != L // 2]):
        ag[k] = rc(out.at[slot], out.at[slot], s_ag.at[k], r_ag.at[k], {"loop": to[k]})
        ag[k].start()
    fw = {0: rc(out.at[slot], out.at[slot], s_fw.at[0], r_fw.at[0], c_dev)}
    fw[0].start()

    gsums = jnp.sum(dnf * xh, axis=0, keepdims=True)
    for i in range(8):
        gsum[0, i : i + 1, :] = gsums[:, i * (width // 8) : (i + 1) * (width // 8)]
    ga = rc(gsum.at[0], gx, s_g.at[0], r_g.at[0], x_dev)
    ga.start()
    ga.wait()
    gsum[1] = gsum[0] + gx[...]
    gb = rc(gsum.at[1], gc, s_g.at[1], r_g.at[1], c_dev)
    gb.start()
    gb.wait()
    gz[l] = gsum[1] + gc[...]
    gcopies = []
    for k in range(1, L):
        gcopies.append(rc(gz.at[l], gz.at[l], s_gz.at[k], r_gz.at[k], {"loop": to[k]}))
        gcopies[-1].start()

    for k in range(1, L):
        ag[k].wait()
        got = 2 * frm[k] + f
        fw[k] = rc(out.at[got], out.at[got], s_fw.at[k], r_fw.at[k], c_dev)
        fw[k].start()
    for copy in gcopies:
        copy.wait()
    acc = gz[0]
    for j in range(1, L):
        acc = acc + gz[j]
    g_gains[...] = acc
    for k in range(L):
        fw[k].wait()


def on_device_fused(L, activations, cotangent, weights_in, weights_down, norm_gains):
    tok, width = activations.shape
    hidden, half = weights_down.shape
    ch = tok // (2 * L)
    pad = ((0, HP - hidden), (0, 0))
    wgu = jnp.concatenate([jnp.pad(weights_in[:, 0], pad), jnp.pad(weights_in[:, 1], pad)], axis=0)
    wd = jnp.pad(weights_down, pad)
    bf, f32 = jnp.bfloat16, jnp.float32
    vm, sem = pltpu.VMEM, pltpu.SemaphoreType.DMA
    spec = pl.BlockSpec(memory_space=pltpu.VMEM)
    shape = jax.ShapeDtypeStruct
    g_gate, g_up, g_down, g_gains, out = pl.pallas_call(
        functools.partial(fused_kernel, L),
        out_shape=(
            shape((hidden, half), f32), shape((hidden, half), f32), shape((hidden, half), f32),
            shape((8, width // 8), f32), shape((2 * L, ch, width), bf),
        ),
        in_specs=[spec] * 5,
        out_specs=(spec,) * 5,
        scratch_shapes=[
            vm((tok, width), bf), vm((tok, width), f32), vm((tok, 128), f32), vm((tok, width), f32),
            vm((2, tok, half), bf),
            vm((2, 3, tok, HP), f32), vm((4, 3, tok, HP), bf),
            vm((2, tok, 2 * HP), bf), vm((2, tok, HP), bf),
            vm((2, tok, half), f32), vm((2, L, ch, half), bf), vm((2, L, ch, half), bf),
            vm((2, ch, half), f32), vm((L, 2, ch, half), bf), vm((L, 2, ch, half), bf),
            vm((ch, half), bf), vm((ch, half), bf), vm((ch, width), f32),
            vm((2, 8, width // 8), f32), vm((8, width // 8), f32), vm((8, width // 8), f32),
            vm((L, 8, width // 8), f32),
            sem((2,)), sem((2,)), sem((2,)), sem((2,)), sem((2,)), sem((2,)), sem((2,)), sem((2,)),
            sem((L, 2)), sem((L, 2)), sem((1,)), sem((1,)),
            sem((L,)), sem((L,)), sem((L,)), sem((L,)), sem((2,)), sem((2,)), sem((L,)), sem((L,)),
        ],
        compiler_params=pltpu.CompilerParams(
            collective_id=0, has_side_effects=True, vmem_limit_bytes=58 * 2**20
        ),
    )(activations, cotangent, wgu, wd, norm_gains[None, :])
    return (
        jnp.stack([g_gate, g_up], axis=1), g_down, g_gains.reshape(width), out.reshape(tok, width),
    )


def body_for(mesh, args_tok, hidden):
    L = mesh.shape["loop"]
    fits = hidden <= HP and mesh.shape["dp"] == 2 and mesh.shape["fsdp"] == 2 and args_tok % (16 * L) == 0
    return functools.partial(on_device_fused, L) if fits and L > 1 else on_device


def solution(mesh):
    def run(activations, cotangent, weights_in, weights_down, norm_gains):
        tok = activations.shape[0] // (mesh.shape["groups"] * mesh.shape["dp"])
        hidden = weights_down.shape[0] // (mesh.shape["loop"] * mesh.shape["fsdp"])
        return mapped(mesh, body_for(mesh, tok, hidden))(
            activations, cotangent, weights_in, weights_down, norm_gains
        )

    return run


def mapped(mesh, body):
    return jax.shard_map(
        body,
        mesh=mesh,
        in_specs=(
            P(("groups", "dp"), None),
            P(("groups", "dp"), None),
            P(("loop", "fsdp"), None, "dp"),
            P(("loop", "fsdp"), "dp"),
            P(),
        ),
        out_specs=(
            P(("groups", "loop", "fsdp"), None, "dp"),
            P(("groups", "loop", "fsdp"), "dp"),
            P("groups"),
            P(("groups", "dp"), None),
        ),
        check_vma=False,
    )
```

```python
import functools

import jax
import jax.numpy as jnp
from jax import lax
from jax.experimental import pallas as pl
from jax.experimental.pallas import tpu as pltpu
from jax.sharding import PartitionSpec as P

EPSILON = 1e-05


def contract_rows(left, right):
    return lax.dot_general(
        left, right, (((0,), (0,)), ((), ())), preferred_element_type=jnp.float32
    )


def input_grad(d_normed, x_hat, inv_rms, cotangent, norm_gains):
    scaled = d_normed * norm_gains
    return (
        cotangent.astype(jnp.float32)
        + inv_rms * (scaled - x_hat * jnp.mean(scaled * x_hat, axis=-1, keepdims=True))
    ).astype(jnp.bfloat16)


def on_device(activations, cotangent, weights_in, weights_down, norm_gains):
    x_float = activations.astype(jnp.float32)
    inv_rms = lax.rsqrt(jnp.mean(x_float * x_float, axis=-1, keepdims=True) + EPSILON)
    x_hat = x_float * inv_rms
    normed = (x_hat * norm_gains).astype(jnp.bfloat16)
    full_in, full_down = (
        lax.all_gather(weights_in, "dp", axis=2, tiled=True),
        lax.all_gather(weights_down, "dp", axis=1, tiled=True),
    )
    gate_val = jnp.dot(normed, full_in[:, 0, :].T, preferred_element_type=jnp.float32)
    up_val = jnp.dot(normed, full_in[:, 1, :].T, preferred_element_type=jnp.float32)
    d_hidden = jnp.dot(cotangent, full_down.T, preferred_element_type=jnp.float32)
    sigma = jax.nn.sigmoid(gate_val)
    silu_val = gate_val * sigma
    hidden = (silu_val * up_val).astype(jnp.bfloat16)
    d_gate = (d_hidden * up_val * sigma * (1.0 + gate_val * (1.0 - sigma))).astype(jnp.bfloat16)
    d_up = (d_hidden * silu_val).astype(jnp.bfloat16)
    partial_normed = jnp.dot(
        d_gate, full_in[:, 0, :], preferred_element_type=jnp.float32
    ) + jnp.dot(d_up, full_in[:, 1, :], preferred_element_type=jnp.float32)
    d_normed = lax.psum(partial_normed, ("loop", "fsdp"))
    grad_gains = lax.psum(jnp.sum(d_normed * x_hat, axis=0), "dp")
    grad_act = input_grad(d_normed, x_hat, inv_rms, cotangent, norm_gains)
    term = jnp.stack(
        [
            contract_rows(d_gate, normed),
            contract_rows(d_up, normed),
            contract_rows(hidden, cotangent),
        ],
        axis=1,
    )
    term = lax.optimization_barrier(term.astype(jnp.bfloat16)).astype(jnp.float32)
    summed = lax.psum_scatter(
        term.astype(jnp.bfloat16), "dp", scatter_dimension=2, tiled=True
    ).astype(jnp.float32)
    return (summed[:, 0:2, :], summed[:, 2, :], grad_gains, grad_act)


HP = 128


def dot_t(left, right):
    return lax.dot_general(
        left, right, (((1,), (1,)), ((), ())), preferred_element_type=jnp.float32
    )


def fused_kernel(
    L, act, cot, w_in, w_down, gains,
    g_gate, g_up, g_down, g_gains, out,
    wgu, wd, normed, xhat, inv_s, cotf, tok_x, part, part_x, dgu, hid,
    dn, p_buf, r_buf, qf, q_buf, rz, t_buf, t_x, fin, gsum, gx, gc, gz,
    s_x, r_x, s_c, r_c, s_p, r_p, s_d, r_d, s_z, r_z, s_t, r_t,
    s_ag, r_ag, s_fw, r_fw, s_g, r_g, s_gz, r_gz,
):
    tok, width = act.shape
    half = width // 2
    hb = tok // 2
    ch = tok // (2 * L)
    l, d, f = lax.axis_index("loop"), lax.axis_index("dp"), lax.axis_index("fsdp")
    mine = pl.ds(pl.multiple_of(d * half, 128), half)
    theirs = pl.ds(pl.multiple_of((1 - d) * half, 128), half)
    x_dev, c_dev = {"dp": 1 - d}, {"fsdp": 1 - f}
    to = [lax.rem(l + k, L) for k in range(L)]

    def rc(src, dst, ss, rs, dev):
        return pltpu.make_async_remote_copy(
            src_ref=src, dst_ref=dst, send_sem=ss, recv_sem=rs,
            device_id=dev, device_id_type=pl.DeviceIdType.MESH,
        )

    barrier = pltpu.get_barrier_semaphore()
    for dev in [x_dev, c_dev] + [{"loop": to[k]} for k in range(1, L)]:
        pl.semaphore_signal(barrier, inc=1, device_id=dev, device_id_type=pl.DeviceIdType.MESH)
    pl.semaphore_wait(barrier, L + 1)

    my_rows = pl.ds(pl.multiple_of(f * hb, 16), hb)
    x_cot = rc(cot.at[my_rows, theirs], tok_x.at[1, my_rows], s_x.at[1], r_x.at[1], x_dev)
    x_cot.start()

    def norm_rows(start):
        def body(i, carry):
            rows = pl.ds(pl.multiple_of(start + i * 16, 16), 16)
            x = act[rows, :].astype(jnp.float32)
            inv = lax.rsqrt(jnp.mean(x * x, axis=-1, keepdims=True) + EPSILON)
            xh = x * inv
            xhat[rows, :] = xh
            inv_s[rows, :] = jnp.broadcast_to(inv, (16, 128))
            normed[rows, :] = (xh * gains[...]).astype(jnp.bfloat16)
            return carry

        lax.fori_loop(0, hb // 16, body, 0)

    norm_rows(f * hb)
    x_nrm = rc(normed.at[my_rows, theirs], tok_x.at[0, my_rows], s_x.at[0], r_x.at[0], x_dev)
    x_nrm.start()
    norm_rows((1 - f) * hb)
    hidden = w_down.shape[0]
    low = hidden // 16 * 16
    for base, dst, src in ((0, wgu, w_in.at[0]), (HP, wgu, w_in.at[1]), (0, wd, w_down)):
        if low < HP:
            dst[base + low : base + HP] = jnp.zeros((HP - low, half), jnp.bfloat16)
        dst[base : base + hidden] = src[...]

    part[0, 2] = dot_t(cot[:, mine], wd[...])
    gu = dot_t(normed[:, mine], wgu[...])
    part[0, 0] = gu[:, :HP]
    part[0, 1] = gu[:, HP:]
    part_x[0] = part[0].astype(jnp.bfloat16)
    p_own = rc(part_x.at[0], part_x.at[3], s_p.at[0], r_p.at[0], x_dev)
    p_own.start()

    def cot_body(i, carry):
        rows = pl.ds(pl.multiple_of(i * 16, 16), 16)
        cotf[rows, :] = cot[rows, :].astype(jnp.float32)
        return carry

    lax.fori_loop(0, tok // 16, cot_body, 0)

    x_cot.wait()
    c_cot = rc(tok_x.at[1, my_rows], tok_x.at[1, my_rows], s_c.at[1], r_c.at[1], c_dev)
    c_cot.start()
    x_nrm.wait()
    c_nrm = rc(tok_x.at[0, my_rows], tok_x.at[0, my_rows], s_c.at[0], r_c.at[0], c_dev)
    c_nrm.start()
    c_cot.wait()
    part[1, 2] = dot_t(tok_x[1], wd[...])
    c_nrm.wait()
    gu = dot_t(tok_x[0], wgu[...])
    part[1, 0] = gu[:, :HP]
    part[1, 1] = gu[:, HP:]
    part_x[1] = part[1].astype(jnp.bfloat16)
    p_oth = rc(part_x.at[1], part_x.at[2], s_p.at[1], r_p.at[1], x_dev)
    p_oth.start()

    def hidden_grads(t):
        gate = part[t, 0] + part_x[2 + t, 0].astype(jnp.float32)
        up = part[t, 1] + part_x[2 + t, 1].astype(jnp.float32)
        dh = part[t, 2] + part_x[2 + t, 2].astype(jnp.float32)
        sig = jax.nn.sigmoid(gate)
        silu = gate * sig
        hid[t] = (silu * up).astype(jnp.bfloat16)
        dgu[t, :, :HP] = (dh * up * sig * (1.0 + gate * (1.0 - sig))).astype(jnp.bfloat16)
        dgu[t, :, HP:] = (dh * silu).astype(jnp.bfloat16)

        def body(i, carry):
            cols = pl.ds(pl.multiple_of(i * 512, 128), 512)
            dn[t, :, cols] = jnp.dot(
                dgu[t], wgu[:, cols], preferred_element_type=jnp.float32
            )
            return carry

        lax.fori_loop(0, half // 512, body, 0)
        for j in range(L):
            rows = pl.ds(pl.multiple_of((2 * j + 1 - f) * ch, 8), ch)
            p_buf[t, j] = dn[t, rows, :].astype(jnp.bfloat16)
        copy = rc(p_buf.at[t], r_buf.at[t], s_d.at[t], r_d.at[t], c_dev)
        copy.start()
        return copy

    p_own.wait()
    steps = [(w, t, k) for k in range(L - 1) for w in (0, 1) for t in (1, 0)]
    ahead = [l + 1, l - 1]
    has_next, has_prev = [l < L - 1, l > 0], [l > 0, l < L - 1]

    def target(w, k):
        return L - 1 - k if w == 0 else k

    def beyond(w, j):
        return l < j if w == 0 else l > j

    def own(t, j):
        rows = pl.ds(pl.multiple_of((2 * j + f) * ch, 8), ch)
        return dn[t, rows, :] + r_buf[t, j].astype(jnp.float32)

    def line(w, t, k):
        return rc(
            q_buf.at[w, k, t], rz.at[w, k, t], s_z.at[w, k, t], r_z.at[w, k, t], {"loop": ahead[w]}
        )

    def first_sends(t):
        for k in range(L - 1):
            for w in (0, 1):

                @pl.when(jnp.logical_not(has_prev[w]))
                def _():
                    q_buf[w, k, t] = own(t, target(w, k)).astype(jnp.bfloat16)
                    line(w, t, k).start()

    def pass_on(w, t, k):
        @pl.when(jnp.logical_and(has_prev[w], beyond(w, target(w, k))))
        def _():
            line(w, t, k).wait_recv()
            val = own(t, target(w, k)) + rz[w, k, t].astype(jnp.float32)
            q_buf[w, k, t] = val.astype(jnp.bfloat16)
            line(w, t, k).start()

    d1 = hidden_grads(1)
    d1.wait()
    first_sends(1)
    p_oth.wait()
    d0 = hidden_grads(0)
    d0.wait()
    first_sends(0)

    def wg_body(i, carry):
        cols = pl.ds(pl.multiple_of(i * 256, 128), 256)
        own_cols = pl.ds(pl.multiple_of(d * half + i * 256, 128), 256)
        gu = contract_rows(dgu[0], normed[:, own_cols]) + contract_rows(dgu[1], tok_x[0, :, cols])
        g_gate[:, cols] = gu[:hidden]
        g_up[:, cols] = gu[HP : HP + hidden]
        down = contract_rows(hid[0], cot[:, own_cols]) + contract_rows(hid[1], tok_x[1, :, cols])
        g_down[:, cols] = down[:hidden]
        return carry

    tiles = half // 256
    for k in range(L - 1):
        for w in (0, 1):
            pass_on(w, 1, k)
        for w in (0, 1):
            pass_on(w, 0, k)
        lax.fori_loop(tiles * k // (L - 1), tiles * (k + 1) // (L - 1), wg_body, 0)

    def total(t):
        qf[t] = own(t, l)
        for w, at in ((0, L - 1 - l), (1, l)):

            @pl.when(has_prev[w])
            def _():
                line(w, t, at).wait_recv()
                qf[t] = qf[t] + rz[w, at, t].astype(jnp.float32)

        return qf[t]

    t_buf[...] = total(1).astype(jnp.bfloat16)
    tc = rc(t_buf, t_x, s_t.at[0], r_t.at[0], x_dev)
    tc.start()
    fin[:, mine] = total(0)
    tc.wait()
    fin[:, theirs] = t_x[...].astype(jnp.float32)

    rows = pl.ds(pl.multiple_of((2 * l + f) * ch, 8), ch)
    dnf = fin[...]
    xh = xhat[rows, :]
    scaled = dnf * gains[...]
    mean = jnp.mean(scaled * xh, axis=-1, keepdims=True)
    res = cotf[rows, :] + inv_s[rows, :1] * (scaled - xh * mean)
    slot = 2 * l + f
    out[slot] = res.astype(jnp.bfloat16)

    def chunk(w, k):
        return out.at[2 * (l - k if w == 0 else l + k) + f]

    def has(w, k):
        return l - k >= 0 if w == 0 else l + k < L

    def gather(w, k):
        return rc(chunk(w, k), chunk(w, k), s_ag.at[w, k], r_ag.at[w, k], {"loop": ahead[w]})

    def came(w, k):
        return rc(chunk(w, k), chunk(w, k), s_ag.at[w, k - 1], r_ag.at[w, k - 1], {"loop": ahead[w]})

    def across(w, k):
        return rc(chunk(w, k), chunk(w, k), s_fw.at[w, k], r_fw.at[w, k], c_dev)

    for w in (0, 1):

        @pl.when(has_next[w])
        def _():
            gather(w, 0).start()

    across(0, 0).start()

    gsums = jnp.sum(dnf * xh, axis=0, keepdims=True)
    for i in range(8):
        gsum[0, i : i + 1, :] = gsums[:, i * (width // 8) : (i + 1) * (width // 8)]
    ga = rc(gsum.at[0], gx, s_g.at[0], r_g.at[0], x_dev)
    ga.start()
    ga.wait()
    gsum[1] = gsum[0] + gx[...]
    gb = rc(gsum.at[1], gc, s_g.at[1], r_g.at[1], c_dev)
    gb.start()
    gb.wait()
    gz[l] = gsum[1] + gc[...]
    gcopies = []
    for k in range(1, L):
        gcopies.append(rc(gz.at[l], gz.at[l], s_gz.at[k], r_gz.at[k], {"loop": to[k]}))
        gcopies[-1].start()

    for k in range(1, L):
        for w in (0, 1):

            @pl.when(has(w, k))
            def _():
                came(w, k).wait_recv()
                if k < L - 1:

                    @pl.when(has_next[w])
                    def _():
                        gather(w, k).start()

                across(w, k).start()

    for copy in gcopies:
        copy.wait()
    acc = gz[0]
    for j in range(1, L):
        acc = acc + gz[j]
    g_gains[...] = acc
    across(0, 0).wait()
    for w in (0, 1):
        for k in range(1, L):

            @pl.when(has(w, k))
            def _():
                across(w, k).wait()

        for k in range(L - 1):

            @pl.when(jnp.logical_and(has(w, k), has_next[w]))
            def _():
                gather(w, k).wait_send()

    for w, t, k in steps:

        @pl.when(beyond(w, target(w, k)))
        def _():
            line(w, t, k).wait_send()


def on_device_fused(L, activations, cotangent, weights_in, weights_down, norm_gains):
    tok, width = activations.shape
    hidden, half = weights_down.shape
    ch = tok // (2 * L)
    bf, f32 = jnp.bfloat16, jnp.float32
    vm, sem = pltpu.VMEM, pltpu.SemaphoreType.DMA
    spec = pl.BlockSpec(memory_space=pltpu.VMEM)
    shape = jax.ShapeDtypeStruct
    g_gate, g_up, g_down, g_gains, out = pl.pallas_call(
        functools.partial(fused_kernel, L),
        out_shape=(
            shape((hidden, half), f32), shape((hidden, half), f32), shape((hidden, half), f32),
            shape((8, width // 8), f32), shape((2 * L, ch, width), bf),
        ),
        in_specs=[spec] * 5,
        out_specs=(spec,) * 5,
        scratch_shapes=[
            vm((2 * HP, half), bf), vm((HP, half), bf),
            vm((tok, width), bf), vm((tok, width), f32), vm((tok, 128), f32), vm((tok, width), f32),
            vm((2, tok, half), bf),
            vm((2, 3, tok, HP), f32), vm((4, 3, tok, HP), bf),
            vm((2, tok, 2 * HP), bf), vm((2, tok, HP), bf),
            vm((2, tok, half), f32), vm((2, L, ch, half), bf), vm((2, L, ch, half), bf),
            vm((2, ch, half), f32), vm((2, L - 1, 2, ch, half), bf), vm((2, L - 1, 2, ch, half), bf),
            vm((ch, half), bf), vm((ch, half), bf), vm((ch, width), f32),
            vm((2, 8, width // 8), f32), vm((8, width // 8), f32), vm((8, width // 8), f32),
            vm((L, 8, width // 8), f32),
            sem((2,)), sem((2,)), sem((2,)), sem((2,)), sem((2,)), sem((2,)), sem((2,)), sem((2,)),
            sem((2, L - 1, 2)), sem((2, L - 1, 2)), sem((1,)), sem((1,)),
            sem((2, L)), sem((2, L)), sem((2, L)), sem((2, L)), sem((2,)), sem((2,)), sem((L,)), sem((L,)),
        ],
        compiler_params=pltpu.CompilerParams(
            collective_id=0, has_side_effects=True, vmem_limit_bytes=58 * 2**20
        ),
    )(activations, cotangent, jnp.transpose(weights_in, (1, 0, 2)), weights_down, norm_gains[None, :])
    return (
        jnp.stack([g_gate, g_up], axis=1), g_down, g_gains.reshape(width), out.reshape(tok, width),
    )


def body_for(mesh, args_tok, hidden):
    L = mesh.shape["loop"]
    fits = hidden <= HP and mesh.shape["dp"] == 2 and mesh.shape["fsdp"] == 2 and args_tok % (16 * L) == 0
    return functools.partial(on_device_fused, L) if fits and L > 1 else on_device


def solution(mesh):
    def run(activations, cotangent, weights_in, weights_down, norm_gains):
        tok = activations.shape[0] // (mesh.shape["groups"] * mesh.shape["dp"])
        hidden = weights_down.shape[0] // (mesh.shape["loop"] * mesh.shape["fsdp"])
        return mapped(mesh, body_for(mesh, tok, hidden))(
            activations, cotangent, weights_in, weights_down, norm_gains
        )

    return run


def mapped(mesh, body):
    return jax.shard_map(
        body,
        mesh=mesh,
        in_specs=(
            P(("groups", "dp"), None),
            P(("groups", "dp"), None),
            P(("loop", "fsdp"), None, "dp"),
            P(("loop", "fsdp"), "dp"),
            P(),
        ),
        out_specs=(
            P(("groups", "loop", "fsdp"), None, "dp"),
            P(("groups", "loop", "fsdp"), "dp"),
            P("groups"),
            P(("groups", "dp"), None),
        ),
        check_vma=False,
    )
```

```python
import functools

import jax
import jax.numpy as jnp
from jax import lax
from jax.experimental import pallas as pl
from jax.experimental.pallas import tpu as pltpu
from jax.sharding import PartitionSpec as P

EPSILON = 1e-05


def contract_rows(left, right):
    return lax.dot_general(
        left, right, (((0,), (0,)), ((), ())), preferred_element_type=jnp.float32
    )


def input_grad(d_normed, x_hat, inv_rms, cotangent, norm_gains):
    scaled = d_normed * norm_gains
    return (
        cotangent.astype(jnp.float32)
        + inv_rms * (scaled - x_hat * jnp.mean(scaled * x_hat, axis=-1, keepdims=True))
    ).astype(jnp.bfloat16)


def on_device(activations, cotangent, weights_in, weights_down, norm_gains):
    x_float = activations.astype(jnp.float32)
    inv_rms = lax.rsqrt(jnp.mean(x_float * x_float, axis=-1, keepdims=True) + EPSILON)
    x_hat = x_float * inv_rms
    normed = (x_hat * norm_gains).astype(jnp.bfloat16)
    full_in, full_down = (
        lax.all_gather(weights_in, "dp", axis=2, tiled=True),
        lax.all_gather(weights_down, "dp", axis=1, tiled=True),
    )
    gate_val = jnp.dot(normed, full_in[:, 0, :].T, preferred_element_type=jnp.float32)
    up_val = jnp.dot(normed, full_in[:, 1, :].T, preferred_element_type=jnp.float32)
    d_hidden = jnp.dot(cotangent, full_down.T, preferred_element_type=jnp.float32)
    sigma = jax.nn.sigmoid(gate_val)
    silu_val = gate_val * sigma
    hidden = (silu_val * up_val).astype(jnp.bfloat16)
    d_gate = (d_hidden * up_val * sigma * (1.0 + gate_val * (1.0 - sigma))).astype(jnp.bfloat16)
    d_up = (d_hidden * silu_val).astype(jnp.bfloat16)
    partial_normed = jnp.dot(
        d_gate, full_in[:, 0, :], preferred_element_type=jnp.float32
    ) + jnp.dot(d_up, full_in[:, 1, :], preferred_element_type=jnp.float32)
    d_normed = lax.psum(partial_normed, ("loop", "fsdp"))
    grad_gains = lax.psum(jnp.sum(d_normed * x_hat, axis=0), "dp")
    grad_act = input_grad(d_normed, x_hat, inv_rms, cotangent, norm_gains)
    term = jnp.stack(
        [
            contract_rows(d_gate, normed),
            contract_rows(d_up, normed),
            contract_rows(hidden, cotangent),
        ],
        axis=1,
    )
    term = lax.optimization_barrier(term.astype(jnp.bfloat16)).astype(jnp.float32)
    summed = lax.psum_scatter(
        term.astype(jnp.bfloat16), "dp", scatter_dimension=2, tiled=True
    ).astype(jnp.float32)
    return (summed[:, 0:2, :], summed[:, 2, :], grad_gains, grad_act)


HP = 128


def dot_t(left, right):
    return lax.dot_general(
        left, right, (((1,), (1,)), ((), ())), preferred_element_type=jnp.float32
    )


def fused_kernel(
    L, act, cot, w_in, w_down, gains,
    g_gate, g_up, g_down, g_gains, out,
    wgu, wd, normed, xhat, inv_s, cotf, tok_x, part, part_x, dgu, hid,
    dn, p_buf, r_buf, qf, q_buf, rz, mg, fin, gsum, gx, gc, gz,
    s_x, r_x, s_c, r_c, s_p, r_p, s_d, r_d, s_z, r_z, r_m,
    s_ag, r_ag, s_fw, r_fw, s_g, r_g, s_gz, r_gz,
):
    tok, width = act.shape
    half = width // 2
    hb = tok // 2
    ch = tok // (2 * L)
    l, d, f = lax.axis_index("loop"), lax.axis_index("dp"), lax.axis_index("fsdp")
    mine = pl.ds(pl.multiple_of(d * half, 128), half)
    theirs = pl.ds(pl.multiple_of((1 - d) * half, 128), half)
    x_dev, c_dev = {"dp": 1 - d}, {"fsdp": 1 - f}
    to = [lax.rem(l + k, L) for k in range(L)]

    def rc(src, dst, ss, rs, dev):
        return pltpu.make_async_remote_copy(
            src_ref=src, dst_ref=dst, send_sem=ss, recv_sem=rs,
            device_id=dev, device_id_type=pl.DeviceIdType.MESH,
        )

    peers = [{"loop": to[k]} for k in range(1, L)]
    peers += [{"loop": to[k], "dp": 1 - d} for k in range(1, L)]
    inner = jnp.logical_and(l > 0, l < L - 1)
    outer = jnp.logical_not(inner)
    via = L - 1 - l
    far = jnp.where(l == 1, 3, 0)
    near = 3 - far

    barrier = pltpu.get_barrier_semaphore()
    for dev in [x_dev, c_dev] + peers:
        pl.semaphore_signal(barrier, inc=1, device_id=dev, device_id_type=pl.DeviceIdType.MESH)
    pl.semaphore_wait(barrier, 2 * L)

    my_rows = pl.ds(pl.multiple_of(f * hb, 16), hb)
    x_cot = rc(cot.at[my_rows, theirs], tok_x.at[1, my_rows], s_x.at[1], r_x.at[1], x_dev)
    x_cot.start()

    def norm_rows(start):
        def body(i, carry):
            rows = pl.ds(pl.multiple_of(start + i * 16, 16), 16)
            x = act[rows, :].astype(jnp.float32)
            inv = lax.rsqrt(jnp.mean(x * x, axis=-1, keepdims=True) + EPSILON)
            xh = x * inv
            xhat[rows, :] = xh
            inv_s[rows, :] = jnp.broadcast_to(inv, (16, 128))
            normed[rows, :] = (xh * gains[...]).astype(jnp.bfloat16)
            return carry

        lax.fori_loop(0, hb // 16, body, 0)

    norm_rows(f * hb)
    x_nrm = rc(normed.at[my_rows, theirs], tok_x.at[0, my_rows], s_x.at[0], r_x.at[0], x_dev)
    x_nrm.start()
    norm_rows((1 - f) * hb)
    hidden = w_down.shape[0]
    low = hidden // 16 * 16
    for base, dst, src in ((0, wgu, w_in.at[0]), (HP, wgu, w_in.at[1]), (0, wd, w_down)):
        if low < HP:
            dst[base + low : base + HP] = jnp.zeros((HP - low, half), jnp.bfloat16)
        dst[base : base + hidden] = src[...]

    part[0, 2] = dot_t(cot[:, mine], wd[...])
    gu = dot_t(normed[:, mine], wgu[...])
    part[0, 0] = gu[:, :HP]
    part[0, 1] = gu[:, HP:]
    part_x[0] = part[0].astype(jnp.bfloat16)
    p_own = rc(part_x.at[0], part_x.at[3], s_p.at[0], r_p.at[0], x_dev)
    p_own.start()

    def cot_body(i, carry):
        rows = pl.ds(pl.multiple_of(i * 16, 16), 16)
        cotf[rows, :] = cot[rows, :].astype(jnp.float32)
        return carry

    lax.fori_loop(0, tok // 16, cot_body, 0)

    x_cot.wait()
    c_cot = rc(tok_x.at[1, my_rows], tok_x.at[1, my_rows], s_c.at[1], r_c.at[1], c_dev)
    c_cot.start()
    x_nrm.wait()
    c_nrm = rc(tok_x.at[0, my_rows], tok_x.at[0, my_rows], s_c.at[0], r_c.at[0], c_dev)
    c_nrm.start()
    c_cot.wait()
    part[1, 2] = dot_t(tok_x[1], wd[...])
    c_nrm.wait()
    gu = dot_t(tok_x[0], wgu[...])
    part[1, 0] = gu[:, :HP]
    part[1, 1] = gu[:, HP:]
    part_x[1] = part[1].astype(jnp.bfloat16)
    p_oth = rc(part_x.at[1], part_x.at[2], s_p.at[1], r_p.at[1], x_dev)
    p_oth.start()

    def hidden_grads(t):
        gate = part[t, 0] + part_x[2 + t, 0].astype(jnp.float32)
        up = part[t, 1] + part_x[2 + t, 1].astype(jnp.float32)
        dh = part[t, 2] + part_x[2 + t, 2].astype(jnp.float32)
        sig = jax.nn.sigmoid(gate)
        silu = gate * sig
        hid[t] = (silu * up).astype(jnp.bfloat16)
        dgu[t, :, :HP] = (dh * up * sig * (1.0 + gate * (1.0 - sig))).astype(jnp.bfloat16)
        dgu[t, :, HP:] = (dh * silu).astype(jnp.bfloat16)

        def body(i, carry):
            cols = pl.ds(pl.multiple_of(i * 512, 128), 512)
            dn[t, :, cols] = jnp.dot(
                dgu[t], wgu[:, cols], preferred_element_type=jnp.float32
            )
            return carry

        lax.fori_loop(0, half // 512, body, 0)
        for j in range(L):
            rows = pl.ds(pl.multiple_of((2 * j + 1 - f) * ch, 8), ch)
            p_buf[t, j] = dn[t, rows, :].astype(jnp.bfloat16)
        copy = rc(p_buf.at[t], r_buf.at[t], s_d.at[t], r_d.at[t], c_dev)
        copy.start()
        return copy

    p_own.wait()
    def own(t, j):
        rows = pl.ds(pl.multiple_of((2 * j + f) * ch, 8), ch)
        return dn[t, rows, :] + r_buf[t, j].astype(jnp.float32)

    def place(t, j):
        return {"loop": j, "dp": 1 - d} if t == 1 else {"loop": j}

    def final_send(t, j):
        return rc(q_buf.at[t, j], rz.at[t, l], s_z.at[t, j], r_z.at[t, l], place(t, j))

    def merge_send(t):
        return rc(q_buf.at[t, far], mg.at[t], s_z.at[t, far], r_m.at[t], {"loop": via})

    def scatter(t):
        @pl.when(inner)
        def _():
            q_buf[t, far] = own(t, far).astype(jnp.bfloat16)
            merge_send(t).start()

        for j in (3, 0, 1, 2):
            go = jnp.logical_or(outer, jnp.logical_and(j != far, j != near))
            if t == 0:
                go = jnp.logical_and(go, j != l)

            @pl.when(go)
            def _():
                q_buf[t, j] = own(t, j).astype(jnp.bfloat16)
                final_send(t, j).start()

    def merge(t):
        @pl.when(inner)
        def _():
            merge_send(t).wait_recv()
            val = own(t, near) + mg[t].astype(jnp.float32)
            q_buf[t, near] = val.astype(jnp.bfloat16)
            final_send(t, near).start()

    d1 = hidden_grads(1)
    d1.wait()
    scatter(1)
    p_oth.wait()
    d0 = hidden_grads(0)
    d0.wait()
    scatter(0)

    def wg_body(i, carry):
        cols = pl.ds(pl.multiple_of(i * 256, 128), 256)
        own_cols = pl.ds(pl.multiple_of(d * half + i * 256, 128), 256)
        gu = contract_rows(dgu[0], normed[:, own_cols]) + contract_rows(dgu[1], tok_x[0, :, cols])
        g_gate[:, cols] = gu[:hidden]
        g_up[:, cols] = gu[HP : HP + hidden]
        down = contract_rows(hid[0], cot[:, own_cols]) + contract_rows(hid[1], tok_x[1, :, cols])
        g_down[:, cols] = down[:hidden]
        return carry

    lax.fori_loop(0, half // 256, wg_body, 0)
    merge(1)
    merge(0)

    def total(t):
        if t == 0:
            qf[t] = own(t, l)
        else:
            qf[t] = jnp.zeros((ch, half), jnp.float32)
        for p in range(L):
            got = l != 3 if p == 1 else l != 0 if p == 2 else l >= 0
            if t == 0:
                got = jnp.logical_and(got, l != p)

            @pl.when(got)
            def _():
                rc(
                    q_buf.at[t, 0], rz.at[t, p], s_z.at[t, 0], r_z.at[t, p], x_dev
                ).wait_recv()
                qf[t] = qf[t] + rz[t, p].astype(jnp.float32)

        return qf[t]

    fin[:, theirs] = total(1)
    fin[:, mine] = total(0)

    rows = pl.ds(pl.multiple_of((2 * l + f) * ch, 8), ch)
    dnf = fin[...]
    xh = xhat[rows, :]
    scaled = dnf * gains[...]
    mean = jnp.mean(scaled * xh, axis=-1, keepdims=True)
    res = cotf[rows, :] + inv_s[rows, :1] * (scaled - xh * mean)
    slot = 2 * l + f
    out[slot] = res.astype(jnp.bfloat16)

    def chunk(p):
        return out.at[2 * p + f]

    def hand(p, j, at):
        return rc(chunk(p), chunk(p), s_ag.at[at], r_ag.at[p], {"loop": j})

    def across(p):
        return rc(chunk(p), chunk(p), s_fw.at[p], r_fw.at[p], c_dev)

    for j in (1, 2, 0, 3):

        @pl.when(jnp.logical_and(j != l, jnp.logical_or(outer, j != far)))
        def _():
            hand(l, j, j).start()

    across(l).start()

    gsums = jnp.sum(dnf * xh, axis=0, keepdims=True)
    for i in range(8):
        gsum[0, i : i + 1, :] = gsums[:, i * (width // 8) : (i + 1) * (width // 8)]
    ga = rc(gsum.at[0], gx, s_g.at[0], r_g.at[0], x_dev)
    ga.start()
    ga.wait()
    gsum[1] = gsum[0] + gx[...]
    gb = rc(gsum.at[1], gc, s_g.at[1], r_g.at[1], c_dev)
    gb.start()
    gb.wait()
    gz[l] = gsum[1] + gc[...]
    gcopies = []
    for k in range(1, L):
        gcopies.append(rc(gz.at[l], gz.at[l], s_gz.at[k], r_gz.at[k], {"loop": to[k]}))
        gcopies[-1].start()

    @pl.when(inner)
    def _():
        hand(via, near, far).wait_recv()
        hand(via, near, far).start()
        across(via).start()

    for p in (1, 2, 0, 3):

        @pl.when(jnp.logical_and(p != l, jnp.logical_or(outer, p != via)))
        def _():
            hand(p, near, p).wait_recv()
            across(p).start()

    for copy in gcopies:
        copy.wait()
    acc = gz[0]
    for j in range(1, L):
        acc = acc + gz[j]
    g_gains[...] = acc
    for p in range(L):
        across(p).wait()

        @pl.when(p != l)
        def _():
            hand(l, p, p).wait_send()
            final_send(0, p).wait_send()

        final_send(1, p).wait_send()


def on_device_fused(L, activations, cotangent, weights_in, weights_down, norm_gains):
    tok, width = activations.shape
    hidden, half = weights_down.shape
    ch = tok // (2 * L)
    bf, f32 = jnp.bfloat16, jnp.float32
    vm, sem = pltpu.VMEM, pltpu.SemaphoreType.DMA
    spec = pl.BlockSpec(memory_space=pltpu.VMEM)
    shape = jax.ShapeDtypeStruct
    g_gate, g_up, g_down, g_gains, out = pl.pallas_call(
        functools.partial(fused_kernel, L),
        out_shape=(
            shape((hidden, half), f32), shape((hidden, half), f32), shape((hidden, half), f32),
            shape((8, width // 8), f32), shape((2 * L, ch, width), bf),
        ),
        in_specs=[spec] * 5,
        out_specs=(spec,) * 5,
        scratch_shapes=[
            vm((2 * HP, half), bf), vm((HP, half), bf),
            vm((tok, width), bf), vm((tok, width), f32), vm((tok, 128), f32), vm((tok, width), f32),
            vm((2, tok, half), bf),
            vm((2, 3, tok, HP), f32), vm((4, 3, tok, HP), bf),
            vm((2, tok, 2 * HP), bf), vm((2, tok, HP), bf),
            vm((2, tok, half), f32), vm((2, L, ch, half), bf), vm((2, L, ch, half), bf),
            vm((2, ch, half), f32), vm((2, L, ch, half), bf), vm((2, L, ch, half), bf),
            vm((2, ch, half), bf), vm((ch, width), f32),
            vm((2, 8, width // 8), f32), vm((8, width // 8), f32), vm((8, width // 8), f32),
            vm((L, 8, width // 8), f32),
            sem((2,)), sem((2,)), sem((2,)), sem((2,)), sem((2,)), sem((2,)), sem((2,)), sem((2,)),
            sem((2, L)), sem((2, L)), sem((2,)),
            sem((L,)), sem((L,)), sem((L,)), sem((L,)), sem((2,)), sem((2,)), sem((L,)), sem((L,)),
        ],
        compiler_params=pltpu.CompilerParams(
            collective_id=0, has_side_effects=True, vmem_limit_bytes=58 * 2**20
        ),
    )(activations, cotangent, jnp.transpose(weights_in, (1, 0, 2)), weights_down, norm_gains[None, :])
    return (
        jnp.stack([g_gate, g_up], axis=1), g_down, g_gains.reshape(width), out.reshape(tok, width),
    )


def body_for(mesh, args_tok, hidden):
    L = mesh.shape["loop"]
    fits = hidden <= HP and mesh.shape["dp"] == 2 and mesh.shape["fsdp"] == 2 and args_tok % (16 * L) == 0
    return functools.partial(on_device_fused, L) if fits and L == 4 else on_device


def solution(mesh):
    def run(activations, cotangent, weights_in, weights_down, norm_gains):
        tok = activations.shape[0] // (mesh.shape["groups"] * mesh.shape["dp"])
        hidden = weights_down.shape[0] // (mesh.shape["loop"] * mesh.shape["fsdp"])
        return mapped(mesh, body_for(mesh, tok, hidden))(
            activations, cotangent, weights_in, weights_down, norm_gains
        )

    return run


def mapped(mesh, body):
    return jax.shard_map(
        body,
        mesh=mesh,
        in_specs=(
            P(("groups", "dp"), None),
            P(("groups", "dp"), None),
            P(("loop", "fsdp"), None, "dp"),
            P(("loop", "fsdp"), "dp"),
            P(),
        ),
        out_specs=(
            P(("groups", "loop", "fsdp"), None, "dp"),
            P(("groups", "loop", "fsdp"), "dp"),
            P("groups"),
            P(("groups", "dp"), None),
        ),
        check_vma=False,
    )
```

```python
import functools

import jax
import jax.numpy as jnp
from jax import lax
from jax.experimental import pallas as pl
from jax.experimental.pallas import tpu as pltpu
from jax.sharding import PartitionSpec as P

EPSILON = 1e-05


def contract_rows(left, right):
    return lax.dot_general(
        left, right, (((0,), (0,)), ((), ())), preferred_element_type=jnp.float32
    )


def input_grad(d_normed, x_hat, inv_rms, cotangent, norm_gains):
    scaled = d_normed * norm_gains
    return (
        cotangent.astype(jnp.float32)
        + inv_rms * (scaled - x_hat * jnp.mean(scaled * x_hat, axis=-1, keepdims=True))
    ).astype(jnp.bfloat16)


def on_device(activations, cotangent, weights_in, weights_down, norm_gains):
    x_float = activations.astype(jnp.float32)
    inv_rms = lax.rsqrt(jnp.mean(x_float * x_float, axis=-1, keepdims=True) + EPSILON)
    x_hat = x_float * inv_rms
    normed = (x_hat * norm_gains).astype(jnp.bfloat16)
    full_in, full_down = (
        lax.all_gather(weights_in, "dp", axis=2, tiled=True),
        lax.all_gather(weights_down, "dp", axis=1, tiled=True),
    )
    gate_val = jnp.dot(normed, full_in[:, 0, :].T, preferred_element_type=jnp.float32)
    up_val = jnp.dot(normed, full_in[:, 1, :].T, preferred_element_type=jnp.float32)
    d_hidden = jnp.dot(cotangent, full_down.T, preferred_element_type=jnp.float32)
    sigma = jax.nn.sigmoid(gate_val)
    silu_val = gate_val * sigma
    hidden = (silu_val * up_val).astype(jnp.bfloat16)
    d_gate = (d_hidden * up_val * sigma * (1.0 + gate_val * (1.0 - sigma))).astype(jnp.bfloat16)
    d_up = (d_hidden * silu_val).astype(jnp.bfloat16)
    partial_normed = jnp.dot(
        d_gate, full_in[:, 0, :], preferred_element_type=jnp.float32
    ) + jnp.dot(d_up, full_in[:, 1, :], preferred_element_type=jnp.float32)
    d_normed = lax.psum(partial_normed, ("loop", "fsdp"))
    grad_gains = lax.psum(jnp.sum(d_normed * x_hat, axis=0), "dp")
    grad_act = input_grad(d_normed, x_hat, inv_rms, cotangent, norm_gains)
    term = jnp.stack(
        [
            contract_rows(d_gate, normed),
            contract_rows(d_up, normed),
            contract_rows(hidden, cotangent),
        ],
        axis=1,
    )
    term = lax.optimization_barrier(term.astype(jnp.bfloat16)).astype(jnp.float32)
    summed = lax.psum_scatter(
        term.astype(jnp.bfloat16), "dp", scatter_dimension=2, tiled=True
    ).astype(jnp.float32)
    return (summed[:, 0:2, :], summed[:, 2, :], grad_gains, grad_act)


HP = 128


def dot_t(left, right):
    return lax.dot_general(
        left, right, (((1,), (1,)), ((), ())), preferred_element_type=jnp.float32
    )


def fused_kernel(
    L, act, cot, w_in, w_down, gains,
    g_gate, g_up, g_down, g_gains, out,
    wgu, wd, normed, xhat, inv_s, cotf, tok_x, part, part_x, dgu, hid,
    dn, p_buf, r_buf, qf, q_buf, rz, mg, fin, gsum, gx, gc, gz,
    s_x, r_x, s_c, r_c, s_m, r_m2, s_e, r_e, s_p, r_p, s_d, r_d, s_z, r_z, r_m,
    s_ag, r_ag, s_fw, r_fw, s_g, r_g, s_gz, r_gz,
):
    tok, width = act.shape
    half = width // 2
    ch = tok // (2 * L)
    l, d, f = lax.axis_index("loop"), lax.axis_index("dp"), lax.axis_index("fsdp")
    mine = pl.ds(pl.multiple_of(d * half, 128), half)
    theirs = pl.ds(pl.multiple_of((1 - d) * half, 128), half)
    x_dev, c_dev = {"dp": 1 - d}, {"fsdp": 1 - f}
    to = [lax.rem(l + k, L) for k in range(L)]

    def rc(src, dst, ss, rs, dev):
        return pltpu.make_async_remote_copy(
            src_ref=src, dst_ref=dst, send_sem=ss, recv_sem=rs,
            device_id=dev, device_id_type=pl.DeviceIdType.MESH,
        )

    peers = [{"loop": to[k]} for k in range(1, L)]
    peers += [{"loop": to[k], "dp": 1 - d} for k in range(1, L)]
    inner = jnp.logical_and(l > 0, l < L - 1)
    outer = jnp.logical_not(inner)
    via = L - 1 - l
    far = jnp.where(l == 1, 3, 0)
    near = 3 - far

    barrier = pltpu.get_barrier_semaphore()
    for dev in [x_dev, c_dev] + peers:
        pl.semaphore_signal(barrier, inc=1, device_id=dev, device_id_type=pl.DeviceIdType.MESH)
    pl.semaphore_wait(barrier, 2 * L)

    qt = tok // 4
    pieces = qt // 16
    odd = lax.rem(l, 2)
    mate = l + 1 - 2 * odd
    first = 2 * odd + f
    second = 2 * (1 - odd) + f

    def piece(quarter, n):
        return pl.ds(pl.multiple_of(quarter * qt + n * 16, 16), 16)

    def x_send(a, n):
        src = cot if a == 1 else normed
        rows = piece(first, n)
        return rc(src.at[rows, theirs], tok_x.at[a, rows], s_x.at[a, n], r_x.at[a, n], x_dev)

    def tok_send(a, n, quarter, sems, dev):
        spot = tok_x.at[a, piece(quarter, n)]
        return rc(spot, spot, sems[0].at[a, n], sems[1].at[a, n], dev)

    def to_mate(a, n):
        return tok_send(a, n, first, (s_m, r_m2), {"loop": mate})

    def to_sib(a, n):
        return tok_send(a, n, first, (s_c, r_c), c_dev)

    def to_sib2(a, n):
        return tok_send(a, n, second, (s_e, r_e), c_dev)

    for n in range(pieces):
        x_send(1, n).start()

    def norm_rows(start):
        def body(i, carry):
            rows = pl.ds(pl.multiple_of(start + i * 16, 16), 16)
            x = act[rows, :].astype(jnp.float32)
            inv = lax.rsqrt(jnp.mean(x * x, axis=-1, keepdims=True) + EPSILON)
            xh = x * inv
            xhat[rows, :] = xh
            inv_s[rows, :] = jnp.broadcast_to(inv, (16, 128))
            normed[rows, :] = (xh * gains[...]).astype(jnp.bfloat16)
            return carry

        lax.fori_loop(0, pieces, body, 0)

    norm_rows(first * qt)
    for n in range(pieces):
        x_send(0, n).start()
    for q in range(1, 4):
        norm_rows(lax.rem(first + q, 4) * qt)
    hidden = w_down.shape[0]
    low = hidden // 16 * 16
    for base, dst, src in ((0, wgu, w_in.at[0]), (HP, wgu, w_in.at[1]), (0, wd, w_down)):
        if low < HP:
            dst[base + low : base + HP] = jnp.zeros((HP - low, half), jnp.bfloat16)
        dst[base : base + hidden] = src[...]

    def forward(a):
        for n in range(pieces):
            x_send(a, n).wait_recv()
            to_mate(a, n).start()
            to_sib(a, n).start()

    forward(1)

    part[0, 2] = dot_t(cot[:, mine], wd[...])
    gu = dot_t(normed[:, mine], wgu[...])
    part[0, 0] = gu[:, :HP]
    part[0, 1] = gu[:, HP:]
    part_x[0] = part[0].astype(jnp.bfloat16)
    p_own = rc(part_x.at[0], part_x.at[3], s_p.at[0], r_p.at[0], x_dev)
    p_own.start()

    def cot_body(i, carry):
        rows = pl.ds(pl.multiple_of(i * 16, 16), 16)
        cotf[rows, :] = cot[rows, :].astype(jnp.float32)
        return carry

    lax.fori_loop(0, tok // 16, cot_body, 0)

    forward(0)
    for a in (1, 0):
        for n in range(pieces):
            to_mate(a, n).wait_recv()
            to_sib2(a, n).start()
    for n in range(pieces):
        to_sib(1, n).wait_recv()
        to_sib2(1, n).wait_recv()
    part[1, 2] = dot_t(tok_x[1], wd[...])
    for n in range(pieces):
        to_sib(0, n).wait_recv()
        to_sib2(0, n).wait_recv()
    gu = dot_t(tok_x[0], wgu[...])
    part[1, 0] = gu[:, :HP]
    part[1, 1] = gu[:, HP:]
    part_x[1] = part[1].astype(jnp.bfloat16)
    p_oth = rc(part_x.at[1], part_x.at[2], s_p.at[1], r_p.at[1], x_dev)
    p_oth.start()

    def hidden_grads(t):
        gate = part[t, 0] + part_x[2 + t, 0].astype(jnp.float32)
        up = part[t, 1] + part_x[2 + t, 1].astype(jnp.float32)
        dh = part[t, 2] + part_x[2 + t, 2].astype(jnp.float32)
        sig = jax.nn.sigmoid(gate)
        silu = gate * sig
        hid[t] = (silu * up).astype(jnp.bfloat16)
        dgu[t, :, :HP] = (dh * up * sig * (1.0 + gate * (1.0 - sig))).astype(jnp.bfloat16)
        dgu[t, :, HP:] = (dh * silu).astype(jnp.bfloat16)

        def body(i, carry):
            cols = pl.ds(pl.multiple_of(i * 512, 128), 512)
            dn[t, :, cols] = jnp.dot(
                dgu[t], wgu[:, cols], preferred_element_type=jnp.float32
            )
            return carry

        lax.fori_loop(0, half // 512, body, 0)
        for j in range(L):
            rows = pl.ds(pl.multiple_of((2 * j + 1 - f) * ch, 8), ch)
            p_buf[t, j] = dn[t, rows, :].astype(jnp.bfloat16)
        copy = rc(p_buf.at[t], r_buf.at[t], s_d.at[t], r_d.at[t], c_dev)
        copy.start()
        return copy

    p_own.wait()
    def own(t, j):
        rows = pl.ds(pl.multiple_of((2 * j + f) * ch, 8), ch)
        return dn[t, rows, :] + r_buf[t, j].astype(jnp.float32)

    def place(t, j):
        return {"loop": j, "dp": 1 - d} if t == 1 else {"loop": j}

    def final_send(t, j):
        return rc(q_buf.at[t, j], rz.at[t, l], s_z.at[t, j], r_z.at[t, l], place(t, j))

    def merge_send(t):
        return rc(q_buf.at[t, far], mg.at[t], s_z.at[t, far], r_m.at[t], {"loop": via})

    def scatter(t):
        @pl.when(inner)
        def _():
            q_buf[t, far] = own(t, far).astype(jnp.bfloat16)
            merge_send(t).start()

        for j in (3, 0, 1, 2):
            go = jnp.logical_or(outer, jnp.logical_and(j != far, j != near))
            if t == 0:
                go = jnp.logical_and(go, j != l)

            @pl.when(go)
            def _():
                q_buf[t, j] = own(t, j).astype(jnp.bfloat16)
                final_send(t, j).start()

    def merge(t):
        @pl.when(inner)
        def _():
            merge_send(t).wait_recv()
            val = own(t, near) + mg[t].astype(jnp.float32)
            q_buf[t, near] = val.astype(jnp.bfloat16)
            final_send(t, near).start()

    d1 = hidden_grads(1)
    d1.wait()
    scatter(1)
    p_oth.wait()
    d0 = hidden_grads(0)
    d0.wait()
    scatter(0)

    def wg_body(i, carry):
        cols = pl.ds(pl.multiple_of(i * 256, 128), 256)
        own_cols = pl.ds(pl.multiple_of(d * half + i * 256, 128), 256)
        gu = contract_rows(dgu[0], normed[:, own_cols]) + contract_rows(dgu[1], tok_x[0, :, cols])
        g_gate[:, cols] = gu[:hidden]
        g_up[:, cols] = gu[HP : HP + hidden]
        down = contract_rows(hid[0], cot[:, own_cols]) + contract_rows(hid[1], tok_x[1, :, cols])
        g_down[:, cols] = down[:hidden]
        return carry

    lax.fori_loop(0, half // 256, wg_body, 0)
    merge(1)
    merge(0)

    def total(t):
        if t == 0:
            qf[t] = own(t, l)
        else:
            qf[t] = jnp.zeros((ch, half), jnp.float32)
        for p in range(L):
            got = l != 3 if p == 1 else l != 0 if p == 2 else l >= 0
            if t == 0:
                got = jnp.logical_and(got, l != p)

            @pl.when(got)
            def _():
                rc(
                    q_buf.at[t, 0], rz.at[t, p], s_z.at[t, 0], r_z.at[t, p], x_dev
                ).wait_recv()
                qf[t] = qf[t] + rz[t, p].astype(jnp.float32)

        return qf[t]

    fin[:, theirs] = total(1)
    fin[:, mine] = total(0)

    rows = pl.ds(pl.multiple_of((2 * l + f) * ch, 8), ch)
    dnf = fin[...]
    xh = xhat[rows, :]
    scaled = dnf * gains[...]
    mean = jnp.mean(scaled * xh, axis=-1, keepdims=True)
    res = cotf[rows, :] + inv_s[rows, :1] * (scaled - xh * mean)
    slot = 2 * l + f
    out[slot] = res.astype(jnp.bfloat16)

    def chunk(p):
        return out.at[2 * p + f]

    def hand(p, j, at):
        return rc(chunk(p), chunk(p), s_ag.at[at], r_ag.at[p], {"loop": j})

    def across(p):
        return rc(chunk(p), chunk(p), s_fw.at[p], r_fw.at[p], c_dev)

    for j in (1, 2, 0, 3):

        @pl.when(jnp.logical_and(j != l, jnp.logical_or(outer, j != far)))
        def _():
            hand(l, j, j).start()

    across(l).start()

    gsums = jnp.sum(dnf * xh, axis=0, keepdims=True)
    for i in range(8):
        gsum[0, i : i + 1, :] = gsums[:, i * (width // 8) : (i + 1) * (width // 8)]
    ga = rc(gsum.at[0], gx, s_g.at[0], r_g.at[0], x_dev)
    ga.start()
    ga.wait()
    gsum[1] = gsum[0] + gx[...]
    gb = rc(gsum.at[1], gc, s_g.at[1], r_g.at[1], c_dev)
    gb.start()
    gb.wait()
    gz[l] = gsum[1] + gc[...]
    gcopies = []
    for k in range(1, L):
        gcopies.append(rc(gz.at[l], gz.at[l], s_gz.at[k], r_gz.at[k], {"loop": to[k]}))
        gcopies[-1].start()

    @pl.when(inner)
    def _():
        hand(via, near, far).wait_recv()
        hand(via, near, far).start()
        across(via).start()

    for p in (1, 2, 0, 3):

        @pl.when(jnp.logical_and(p != l, jnp.logical_or(outer, p != via)))
        def _():
            hand(p, near, p).wait_recv()
            across(p).start()

    for copy in gcopies:
        copy.wait()
    acc = gz[0]
    for j in range(1, L):
        acc = acc + gz[j]
    g_gains[...] = acc
    for a in (1, 0):
        for n in range(pieces):
            x_send(a, n).wait_send()
            to_mate(a, n).wait_send()
            to_sib(a, n).wait_send()
            to_sib2(a, n).wait_send()
    for p in range(L):
        across(p).wait()

        @pl.when(p != l)
        def _():
            hand(l, p, p).wait_send()
            final_send(0, p).wait_send()

        final_send(1, p).wait_send()


def on_device_fused(L, activations, cotangent, weights_in, weights_down, norm_gains):
    tok, width = activations.shape
    hidden, half = weights_down.shape
    ch = tok // (2 * L)
    bf, f32 = jnp.bfloat16, jnp.float32
    vm, sem = pltpu.VMEM, pltpu.SemaphoreType.DMA
    spec = pl.BlockSpec(memory_space=pltpu.VMEM)
    shape = jax.ShapeDtypeStruct
    g_gate, g_up, g_down, g_gains, out = pl.pallas_call(
        functools.partial(fused_kernel, L),
        out_shape=(
            shape((hidden, half), f32), shape((hidden, half), f32), shape((hidden, half), f32),
            shape((8, width // 8), f32), shape((2 * L, ch, width), bf),
        ),
        in_specs=[spec] * 5,
        out_specs=(spec,) * 5,
        scratch_shapes=[
            vm((2 * HP, half), bf), vm((HP, half), bf),
            vm((tok, width), bf), vm((tok, width), f32), vm((tok, 128), f32), vm((tok, width), f32),
            vm((2, tok, half), bf),
            vm((2, 3, tok, HP), f32), vm((4, 3, tok, HP), bf),
            vm((2, tok, 2 * HP), bf), vm((2, tok, HP), bf),
            vm((2, tok, half), f32), vm((2, L, ch, half), bf), vm((2, L, ch, half), bf),
            vm((2, ch, half), f32), vm((2, L, ch, half), bf), vm((2, L, ch, half), bf),
            vm((2, ch, half), bf), vm((ch, width), f32),
            vm((2, 8, width // 8), f32), vm((8, width // 8), f32), vm((8, width // 8), f32),
            vm((L, 8, width // 8), f32),
            *[sem((2, tok // 64))] * 8, sem((2,)), sem((2,)), sem((2,)), sem((2,)),
            sem((2, L)), sem((2, L)), sem((2,)),
            sem((L,)), sem((L,)), sem((L,)), sem((L,)), sem((2,)), sem((2,)), sem((L,)), sem((L,)),
        ],
        compiler_params=pltpu.CompilerParams(
            collective_id=0, has_side_effects=True, vmem_limit_bytes=58 * 2**20
        ),
    )(activations, cotangent, jnp.transpose(weights_in, (1, 0, 2)), weights_down, norm_gains[None, :])
    return (
        jnp.stack([g_gate, g_up], axis=1), g_down, g_gains.reshape(width), out.reshape(tok, width),
    )


def body_for(mesh, args_tok, hidden):
    L = mesh.shape["loop"]
    fits = hidden <= HP and mesh.shape["dp"] == 2 and mesh.shape["fsdp"] == 2 and args_tok % 64 == 0
    return functools.partial(on_device_fused, L) if fits and L == 4 else on_device


def solution(mesh):
    def run(activations, cotangent, weights_in, weights_down, norm_gains):
        tok = activations.shape[0] // (mesh.shape["groups"] * mesh.shape["dp"])
        hidden = weights_down.shape[0] // (mesh.shape["loop"] * mesh.shape["fsdp"])
        return mapped(mesh, body_for(mesh, tok, hidden))(
            activations, cotangent, weights_in, weights_down, norm_gains
        )

    return run


def mapped(mesh, body):
    return jax.shard_map(
        body,
        mesh=mesh,
        in_specs=(
            P(("groups", "dp"), None),
            P(("groups", "dp"), None),
            P(("loop", "fsdp"), None, "dp"),
            P(("loop", "fsdp"), "dp"),
            P(),
        ),
        out_specs=(
            P(("groups", "loop", "fsdp"), None, "dp"),
            P(("groups", "loop", "fsdp"), "dp"),
            P("groups"),
            P(("groups", "dp"), None),
        ),
        check_vma=False,
    )
```

```python
import functools

import jax
import jax.numpy as jnp
from jax import lax
from jax.experimental import pallas as pl
from jax.experimental.pallas import tpu as pltpu
from jax.sharding import PartitionSpec as P

EPSILON = 1e-05


def contract_rows(left, right):
    return lax.dot_general(
        left, right, (((0,), (0,)), ((), ())), preferred_element_type=jnp.float32
    )


def input_grad(d_normed, x_hat, inv_rms, cotangent, norm_gains):
    scaled = d_normed * norm_gains
    return (
        cotangent.astype(jnp.float32)
        + inv_rms * (scaled - x_hat * jnp.mean(scaled * x_hat, axis=-1, keepdims=True))
    ).astype(jnp.bfloat16)


def on_device(activations, cotangent, weights_in, weights_down, norm_gains):
    x_float = activations.astype(jnp.float32)
    inv_rms = lax.rsqrt(jnp.mean(x_float * x_float, axis=-1, keepdims=True) + EPSILON)
    x_hat = x_float * inv_rms
    normed = (x_hat * norm_gains).astype(jnp.bfloat16)
    full_in, full_down = (
        lax.all_gather(weights_in, "dp", axis=2, tiled=True),
        lax.all_gather(weights_down, "dp", axis=1, tiled=True),
    )
    gate_val = jnp.dot(normed, full_in[:, 0, :].T, preferred_element_type=jnp.float32)
    up_val = jnp.dot(normed, full_in[:, 1, :].T, preferred_element_type=jnp.float32)
    d_hidden = jnp.dot(cotangent, full_down.T, preferred_element_type=jnp.float32)
    sigma = jax.nn.sigmoid(gate_val)
    silu_val = gate_val * sigma
    hidden = (silu_val * up_val).astype(jnp.bfloat16)
    d_gate = (d_hidden * up_val * sigma * (1.0 + gate_val * (1.0 - sigma))).astype(jnp.bfloat16)
    d_up = (d_hidden * silu_val).astype(jnp.bfloat16)
    partial_normed = jnp.dot(
        d_gate, full_in[:, 0, :], preferred_element_type=jnp.float32
    ) + jnp.dot(d_up, full_in[:, 1, :], preferred_element_type=jnp.float32)
    d_normed = lax.psum(partial_normed, ("loop", "fsdp"))
    grad_gains = lax.psum(jnp.sum(d_normed * x_hat, axis=0), "dp")
    grad_act = input_grad(d_normed, x_hat, inv_rms, cotangent, norm_gains)
    term = jnp.stack(
        [
            contract_rows(d_gate, normed),
            contract_rows(d_up, normed),
            contract_rows(hidden, cotangent),
        ],
        axis=1,
    )
    term = lax.optimization_barrier(term.astype(jnp.bfloat16)).astype(jnp.float32)
    summed = lax.psum_scatter(
        term.astype(jnp.bfloat16), "dp", scatter_dimension=2, tiled=True
    ).astype(jnp.float32)
    return (summed[:, 0:2, :], summed[:, 2, :], grad_gains, grad_act)


HP = 128


def dot_t(left, right):
    return lax.dot_general(
        left, right, (((1,), (1,)), ((), ())), preferred_element_type=jnp.float32
    )


def fused_kernel(
    L, act, cot, w_in, w_down, gains,
    g_in, g_down, g_gains, out,
    wgu, wd, normed, xhat, inv_s, cotf, tok_x, part, part_x, dgu, hid,
    dn, p_buf, r_buf, qf, q_buf, rz, mg, fin, gsum, gx, gc, gz,
    s_x, r_x, s_c, r_c, s_m, r_m2, s_e, r_e, s_p, r_p, s_d, r_d, s_z, r_z, r_m,
    s_ag, r_ag, s_fw, r_fw, s_g, r_g, s_gz, r_gz,
):
    tok, width = act.shape
    half = width // 2
    ch = tok // (2 * L)
    l, d, f = lax.axis_index("loop"), lax.axis_index("dp"), lax.axis_index("fsdp")
    mine = pl.ds(pl.multiple_of(d * half, 128), half)
    theirs = pl.ds(pl.multiple_of((1 - d) * half, 128), half)
    x_dev, c_dev = {"dp": 1 - d}, {"fsdp": 1 - f}
    to = [lax.rem(l + k, L) for k in range(L)]

    def rc(src, dst, ss, rs, dev):
        return pltpu.make_async_remote_copy(
            src_ref=src, dst_ref=dst, send_sem=ss, recv_sem=rs,
            device_id=dev, device_id_type=pl.DeviceIdType.MESH,
        )

    peers = [{"loop": to[k]} for k in range(1, L)]
    peers += [{"loop": to[k], "dp": 1 - d} for k in range(1, L)]
    inner = jnp.logical_and(l > 0, l < L - 1)
    outer = jnp.logical_not(inner)
    via = L - 1 - l
    far = jnp.where(l == 1, 3, 0)
    near = 3 - far

    barrier = pltpu.get_barrier_semaphore()
    for dev in [x_dev, c_dev] + peers:
        pl.semaphore_signal(barrier, inc=1, device_id=dev, device_id_type=pl.DeviceIdType.MESH)
    pl.semaphore_wait(barrier, 2 * L)

    qt = tok // 4
    pieces = qt // 16
    odd = lax.rem(l, 2)
    mate = l + 1 - 2 * odd
    first = 2 * odd + f
    second = 2 * (1 - odd) + f

    def piece(quarter, n):
        return pl.ds(pl.multiple_of(quarter * qt + n * 16, 16), 16)

    def x_send(a, n):
        src = cot if a == 1 else normed
        rows = piece(first, n)
        return rc(src.at[rows, theirs], tok_x.at[a, rows], s_x.at[a, n], r_x.at[a, n], x_dev)

    def tok_send(a, n, quarter, sems, dev):
        spot = tok_x.at[a, piece(quarter, n)]
        return rc(spot, spot, sems[0].at[a, n], sems[1].at[a, n], dev)

    def to_mate(a, n):
        return tok_send(a, n, first, (s_m, r_m2), {"loop": mate})

    def to_sib(a, n):
        return tok_send(a, n, first, (s_c, r_c), c_dev)

    def to_sib2(a, n):
        return tok_send(a, n, second, (s_e, r_e), c_dev)

    for n in range(pieces):
        x_send(1, n).start()

    def norm_rows(start):
        def body(i, carry):
            rows = pl.ds(pl.multiple_of(start + i * 16, 16), 16)
            x = act[rows, :].astype(jnp.float32)
            inv = lax.rsqrt(jnp.mean(x * x, axis=-1, keepdims=True) + EPSILON)
            xh = x * inv
            xhat[rows, :] = xh
            inv_s[rows, :] = jnp.broadcast_to(inv, (16, 128))
            normed[rows, :] = (xh * gains[...]).astype(jnp.bfloat16)
            return carry

        lax.fori_loop(0, pieces, body, 0)

    norm_rows(first * qt)
    for n in range(pieces):
        x_send(0, n).start()
    for q in range(1, 4):
        norm_rows(lax.rem(first + q, 4) * qt)
    hidden = w_down.shape[0]
    low = hidden // 16 * 16
    for base, dst, src in ((0, wgu, w_in.at[0]), (HP, wgu, w_in.at[1]), (0, wd, w_down)):
        if low < HP:
            dst[base + low : base + HP] = jnp.zeros((HP - low, half), jnp.bfloat16)
        dst[base : base + hidden] = src[...]

    def forward(a):
        for n in range(pieces):
            x_send(a, n).wait_recv()
            to_mate(a, n).start()
            to_sib(a, n).start()

    forward(1)

    part[0, 2] = dot_t(cot[:, mine], wd[...])
    gu = dot_t(normed[:, mine], wgu[...])
    part[0, 0] = gu[:, :HP]
    part[0, 1] = gu[:, HP:]
    part_x[0] = part[0].astype(jnp.bfloat16)
    p_own = rc(part_x.at[0], part_x.at[3], s_p.at[0], r_p.at[0], x_dev)
    p_own.start()

    def cot_body(i, carry):
        rows = pl.ds(pl.multiple_of(i * 16, 16), 16)
        cotf[rows, :] = cot[rows, :].astype(jnp.float32)
        return carry

    lax.fori_loop(0, tok // 16, cot_body, 0)

    forward(0)
    for a in (1, 0):
        for n in range(pieces):
            to_mate(a, n).wait_recv()
            to_sib2(a, n).start()
    for n in range(pieces):
        to_sib(1, n).wait_recv()
        to_sib2(1, n).wait_recv()
    part[1, 2] = dot_t(tok_x[1], wd[...])
    for n in range(pieces):
        to_sib(0, n).wait_recv()
        to_sib2(0, n).wait_recv()
    gu = dot_t(tok_x[0], wgu[...])
    part[1, 0] = gu[:, :HP]
    part[1, 1] = gu[:, HP:]
    part_x[1] = part[1].astype(jnp.bfloat16)
    p_oth = rc(part_x.at[1], part_x.at[2], s_p.at[1], r_p.at[1], x_dev)
    p_oth.start()

    def hidden_grads(t):
        gate = part[t, 0] + part_x[2 + t, 0].astype(jnp.float32)
        up = part[t, 1] + part_x[2 + t, 1].astype(jnp.float32)
        dh = part[t, 2] + part_x[2 + t, 2].astype(jnp.float32)
        sig = jax.nn.sigmoid(gate)
        silu = gate * sig
        hid[t] = (silu * up).astype(jnp.bfloat16)
        dgu[t, :, :HP] = (dh * up * sig * (1.0 + gate * (1.0 - sig))).astype(jnp.bfloat16)
        dgu[t, :, HP:] = (dh * silu).astype(jnp.bfloat16)

        def body(i, carry):
            cols = pl.ds(pl.multiple_of(i * 512, 128), 512)
            dn[t, :, cols] = jnp.dot(
                dgu[t], wgu[:, cols], preferred_element_type=jnp.float32
            )
            return carry

        lax.fori_loop(0, half // 512, body, 0)
        for j in range(L):
            rows = pl.ds(pl.multiple_of((2 * j + 1 - f) * ch, 8), ch)
            p_buf[t, j] = dn[t, rows, :].astype(jnp.bfloat16)
        copy = rc(p_buf.at[t], r_buf.at[t], s_d.at[t], r_d.at[t], c_dev)
        copy.start()
        return copy

    p_own.wait()
    def own(t, j):
        rows = pl.ds(pl.multiple_of((2 * j + f) * ch, 8), ch)
        return dn[t, rows, :] + r_buf[t, j].astype(jnp.float32)

    def place(t, j):
        return {"loop": j, "dp": 1 - d} if t == 1 else {"loop": j}

    def final_send(t, j):
        return rc(q_buf.at[t, j], rz.at[t, l], s_z.at[t, j], r_z.at[t, l], place(t, j))

    def merge_send(t):
        return rc(q_buf.at[t, far], mg.at[t], s_z.at[t, far], r_m.at[t], {"loop": via})

    def scatter(t):
        @pl.when(inner)
        def _():
            q_buf[t, far] = own(t, far).astype(jnp.bfloat16)
            merge_send(t).start()

        for j in (3, 0, 1, 2):
            go = jnp.logical_or(outer, jnp.logical_and(j != far, j != near))
            if t == 0:
                go = jnp.logical_and(go, j != l)

            @pl.when(go)
            def _():
                q_buf[t, j] = own(t, j).astype(jnp.bfloat16)
                final_send(t, j).start()

    def merge(t):
        @pl.when(inner)
        def _():
            merge_send(t).wait_recv()
            val = own(t, near) + mg[t].astype(jnp.float32)
            q_buf[t, near] = val.astype(jnp.bfloat16)
            final_send(t, near).start()

    d1 = hidden_grads(1)
    d1.wait()
    scatter(1)
    p_oth.wait()
    d0 = hidden_grads(0)
    d0.wait()
    scatter(0)

    def wg_body(i, carry):
        cols = pl.ds(pl.multiple_of(i * 256, 128), 256)
        own_cols = pl.ds(pl.multiple_of(d * half + i * 256, 128), 256)
        gu = contract_rows(dgu[0], normed[:, own_cols]) + contract_rows(dgu[1], tok_x[0, :, cols])
        g_in[:, 0, cols] = gu[:hidden]
        g_in[:, 1, cols] = gu[HP : HP + hidden]
        down = contract_rows(hid[0], cot[:, own_cols]) + contract_rows(hid[1], tok_x[1, :, cols])
        g_down[:, cols] = down[:hidden]
        return carry

    lax.fori_loop(0, half // 256, wg_body, 0)
    merge(1)
    merge(0)

    def total(t):
        if t == 0:
            qf[t] = own(t, l)
        else:
            qf[t] = jnp.zeros((ch, half), jnp.float32)
        for p in range(L):
            got = l != 3 if p == 1 else l != 0 if p == 2 else l >= 0
            if t == 0:
                got = jnp.logical_and(got, l != p)

            @pl.when(got)
            def _():
                rc(
                    q_buf.at[t, 0], rz.at[t, p], s_z.at[t, 0], r_z.at[t, p], x_dev
                ).wait_recv()
                qf[t] = qf[t] + rz[t, p].astype(jnp.float32)

        return qf[t]

    fin[:, theirs] = total(1)
    fin[:, mine] = total(0)

    rows = pl.ds(pl.multiple_of((2 * l + f) * ch, 8), ch)
    dnf = fin[...]
    xh = xhat[rows, :]
    scaled = dnf * gains[...]
    mean = jnp.mean(scaled * xh, axis=-1, keepdims=True)
    res = cotf[rows, :] + inv_s[rows, :1] * (scaled - xh * mean)
    slot = 2 * l + f
    out[slot] = res.astype(jnp.bfloat16)

    def chunk(p):
        return out.at[2 * p + f]

    def hand(p, j, at):
        return rc(chunk(p), chunk(p), s_ag.at[at], r_ag.at[p], {"loop": j})

    def across(p):
        return rc(chunk(p), chunk(p), s_fw.at[p], r_fw.at[p], c_dev)

    for j in (1, 2, 0, 3):

        @pl.when(jnp.logical_and(j != l, jnp.logical_or(outer, j != far)))
        def _():
            hand(l, j, j).start()

    across(l).start()

    gsums = jnp.sum(dnf * xh, axis=0, keepdims=True)
    for i in range(8):
        gsum[0, i : i + 1, :] = gsums[:, i * (width // 8) : (i + 1) * (width // 8)]
    ga = rc(gsum.at[0], gx, s_g.at[0], r_g.at[0], x_dev)
    ga.start()
    ga.wait()
    gsum[1] = gsum[0] + gx[...]
    gb = rc(gsum.at[1], gc, s_g.at[1], r_g.at[1], c_dev)
    gb.start()
    gb.wait()
    gz[l] = gsum[1] + gc[...]
    gcopies = []
    for k in range(1, L):
        gcopies.append(rc(gz.at[l], gz.at[l], s_gz.at[k], r_gz.at[k], {"loop": to[k]}))
        gcopies[-1].start()

    @pl.when(inner)
    def _():
        hand(via, near, far).wait_recv()
        hand(via, near, far).start()
        across(via).start()

    for p in (1, 2, 0, 3):

        @pl.when(jnp.logical_and(p != l, jnp.logical_or(outer, p != via)))
        def _():
            hand(p, near, p).wait_recv()
            across(p).start()

    for copy in gcopies:
        copy.wait()
    acc = gz[0]
    for j in range(1, L):
        acc = acc + gz[j]
    g_gains[...] = acc
    for a in (1, 0):
        for n in range(pieces):
            x_send(a, n).wait_send()
            to_mate(a, n).wait_send()
            to_sib(a, n).wait_send()
            to_sib2(a, n).wait_send()
    for p in range(L):
        across(p).wait()

        @pl.when(p != l)
        def _():
            hand(l, p, p).wait_send()
            final_send(0, p).wait_send()

        final_send(1, p).wait_send()


def on_device_fused(L, activations, cotangent, weights_in, weights_down, norm_gains):
    tok, width = activations.shape
    hidden, half = weights_down.shape
    ch = tok // (2 * L)
    bf, f32 = jnp.bfloat16, jnp.float32
    vm, sem = pltpu.VMEM, pltpu.SemaphoreType.DMA
    spec = pl.BlockSpec(memory_space=pltpu.VMEM)
    shape = jax.ShapeDtypeStruct
    g_in, g_down, g_gains, out = pl.pallas_call(
        functools.partial(fused_kernel, L),
        out_shape=(
            shape((hidden, 2, half), f32), shape((hidden, half), f32),
            shape((8, width // 8), f32), shape((2 * L, ch, width), bf),
        ),
        in_specs=[spec] * 5,
        out_specs=(spec,) * 4,
        scratch_shapes=[
            vm((2 * HP, half), bf), vm((HP, half), bf),
            vm((tok, width), bf), vm((tok, width), f32), vm((tok, 128), f32), vm((tok, width), f32),
            vm((2, tok, half), bf),
            vm((2, 3, tok, HP), f32), vm((4, 3, tok, HP), bf),
            vm((2, tok, 2 * HP), bf), vm((2, tok, HP), bf),
            vm((2, tok, half), f32), vm((2, L, ch, half), bf), vm((2, L, ch, half), bf),
            vm((2, ch, half), f32), vm((2, L, ch, half), bf), vm((2, L, ch, half), bf),
            vm((2, ch, half), bf), vm((ch, width), f32),
            vm((2, 8, width // 8), f32), vm((8, width // 8), f32), vm((8, width // 8), f32),
            vm((L, 8, width // 8), f32),
            *[sem((2, tok // 64))] * 8, sem((2,)), sem((2,)), sem((2,)), sem((2,)),
            sem((2, L)), sem((2, L)), sem((2,)),
            sem((L,)), sem((L,)), sem((L,)), sem((L,)), sem((2,)), sem((2,)), sem((L,)), sem((L,)),
        ],
        compiler_params=pltpu.CompilerParams(
            collective_id=0, has_side_effects=True, vmem_limit_bytes=58 * 2**20
        ),
    )(activations, cotangent, jnp.transpose(weights_in, (1, 0, 2)), weights_down, norm_gains[None, :])
    return (
        g_in, g_down, g_gains.reshape(width), out.reshape(tok, width),
    )


def body_for(mesh, args_tok, hidden):
    L = mesh.shape["loop"]
    fits = hidden <= HP and mesh.shape["dp"] == 2 and mesh.shape["fsdp"] == 2 and args_tok % 64 == 0
    return functools.partial(on_device_fused, L) if fits and L == 4 else on_device


def solution(mesh):
    def run(activations, cotangent, weights_in, weights_down, norm_gains):
        tok = activations.shape[0] // (mesh.shape["groups"] * mesh.shape["dp"])
        hidden = weights_down.shape[0] // (mesh.shape["loop"] * mesh.shape["fsdp"])
        return mapped(mesh, body_for(mesh, tok, hidden))(
            activations, cotangent, weights_in, weights_down, norm_gains
        )

    return run


def mapped(mesh, body):
    return jax.shard_map(
        body,
        mesh=mesh,
        in_specs=(
            P(("groups", "dp"), None),
            P(("groups", "dp"), None),
            P(("loop", "fsdp"), None, "dp"),
            P(("loop", "fsdp"), "dp"),
            P(),
        ),
        out_specs=(
            P(("groups", "loop", "fsdp"), None, "dp"),
            P(("groups", "loop", "fsdp"), "dp"),
            P("groups"),
            P(("groups", "dp"), None),
        ),
        check_vma=False,
    )
```
